32 devices in a mesh: section: 2 (over y), segment: 4 (over x, core), fsdp: 4 (over z).
Axes of the slice: x: 2, y: 2, z: 4, core: 2. Of those that a mesh axis runs over, the one named last changes fastest.
Arguments:
- out_grad: bfloat16 [2, 4, 256, 6144], P(None, 'fsdp'), may hold values from -48 to 48
- queries: bfloat16 [2, 4, 256, 6144], P(None, 'fsdp', None, 'segment'), may hold values from -40 to 40
- enc_keys: bfloat16 [2, 4, 256, 6144], P(None, 'fsdp', None, 'segment'), may hold values from -4 to 4
- enc_values: bfloat16 [2, 4, 256, 6144], P(None, 'fsdp', None, 'segment'), may hold values from -6 to 6
- key_mask: int32 [2, 4, 256], P(None, 'fsdp'), may hold values from 0 to 1, as said below
- weights: bfloat16 [2, 2, 6144, 6144], P('section', None, 'fsdp', 'segment'), may hold values from -0.078125 to 0.078125
Outputs:
- grads: bfloat16 [2, 2, 4, 256, 6144], P('section', None, 'fsdp', None, 'segment')
The draws below stay inside these ranges and needn't reach their ends.
Inputs may be any that keep to these rules, and one draw needn't show every extreme that they name: `key_mask`: each row is 1 on a prefix of 128 or more positions and 0 after it; the first reaction of every microbatch has no padding.
All inputs are finite; a program needn't handle non-finite values.
Results may differ from the reference program's by a relative error of at most 0.014.
Values may be sent and summed in bfloat16 or wider, within the bound.
A program may use at most 192 MiB of HBM per device.

```python
import jax
import jax.numpy as jnp
from jax import lax

D = 6144
HEADS = 48
HDIM = 128
LEN = 256
MB = 2
BATCH = 4
HEADS_DEV = 12
N_SEGMENT = 4


def query_key_pair(key):
    shaped = (MB, BATCH, LEN, HEADS, HDIM)
    key_draw = jnp.clip(jax.random.normal(jax.random.fold_in(key, 11), shaped, jnp.float32), -4.0, 4.0)
    query_draw = jnp.clip(jax.random.normal(jax.random.fold_in(key, 12), shaped, jnp.float32), -4.0, 4.0)
    return (query_draw.reshape(MB, BATCH, LEN, HEADS * HDIM), key_draw.reshape(MB, BATCH, LEN, HEADS * HDIM))


def draw_queries(key, part):
    return query_key_pair(key)[0].astype(jnp.bfloat16)


def draw_enc_keys(key, part):
    return query_key_pair(key)[1].astype(jnp.bfloat16)


def draw_key_mask(key, part):
    lengths = jax.random.randint(jax.random.fold_in(key, 21), (MB, BATCH), LEN // 2, LEN + 1)
    lengths = lengths.at[:, 0].set(LEN)
    position = jnp.arange(LEN)
    return (position[None, None, :] < lengths[:, :, None]).astype(jnp.int32)


def block_levels(key, extent, split, least, largest):
    loudness, own = 1.0, jax.random.fold_in(key, 6)
    for dim, shards_of in split:
        draws = jnp.exp(jax.random.uniform(jax.random.fold_in(own, dim), (shards_of,), jnp.float32, least / len(split), largest / len(split)))
        loudness = loudness * jnp.repeat(draws, extent[dim] // shards_of).reshape([-1 if axis == dim else 1 for axis in range(len(extent))])
    return loudness


def scatter_about(stream_key, shape, scale, bound, shards=(), held_as=jnp.bfloat16):
    values = jax.random.normal(stream_key, shape, jnp.float32) * scale
    if len(shards) > 0:
        values = block_levels(stream_key, shape, shards, -0.22, 0.18) * values
    return jnp.clip(values, min=-bound, max=bound).astype(held_as)


def setup_inputs(seed: int = 0) -> dict:
    seeds = jax.random.split(jax.random.key(seed), 7)
    out_grad = scatter_about(seeds[0], (MB, BATCH, LEN, D), 8.0, 48.0, ((1, 4),))
    queries = draw_queries(jax.random.fold_in(seeds[6], 71), 0)
    enc_keys = draw_enc_keys(jax.random.fold_in(seeds[6], 71), 0)
    enc_values = scatter_about(seeds[3], (MB, BATCH, LEN, HEADS * HDIM), 1.0, 6.0, ((1, 4), (3, 4)))
    key_mask = draw_key_mask(jax.random.fold_in(seeds[6], 71), 0)
    weights = scatter_about(seeds[5], (2, 2, D, HEADS * HDIM), D ** -0.5, 0.078125, ((0, 2), (2, 4), (3, 4)))
    return dict(out_grad=out_grad, queries=queries, enc_keys=enc_keys, enc_values=enc_values, key_mask=key_mask, weights=weights)


def attention_grads(items):
    ctx_grad, queries, enc_keys, enc_values, key_mask = items
    score_scale = HDIM ** -0.5
    query_all = queries.astype(jnp.float32)
    key_all = enc_keys.astype(jnp.float32)
    value_all = enc_values.astype(jnp.float32)
    grad_all = ctx_grad.astype(jnp.float32)
    scores = jnp.einsum("ihc,jhc->hij", query_all, key_all) * score_scale
    scores = jnp.where(key_mask[None, None, :] > 0, scores, -jnp.inf)
    row_top = jnp.max(scores, axis=-1, keepdims=True)
    exp_scores = jnp.exp(scores - row_top)
    probabilities = exp_scores / jnp.sum(exp_scores, axis=-1, keepdims=True)
    probs_half = lax.optimization_barrier(probabilities.astype(jnp.bfloat16)).astype(jnp.float32)
    prob_grad = jnp.einsum("ihc,jhc->hij", grad_all, value_all)
    center = jnp.sum(probabilities * prob_grad, axis=-1, keepdims=True)
    score_grad = lax.optimization_barrier((probabilities * (prob_grad - center)).astype(jnp.bfloat16)).astype(jnp.float32)
    query_grad = (jnp.einsum("hij,jhc->ihc", score_grad, key_all) * score_scale).astype(jnp.bfloat16)
    key_grad = (jnp.einsum("hij,ihc->jhc", score_grad, query_all) * score_scale).astype(jnp.bfloat16)
    value_grad = jnp.einsum("hij,ihc->jhc", probs_half, grad_all).astype(jnp.bfloat16)
    return query_grad, key_grad, value_grad


def project(grad_rows, weight_cols):
    return jnp.dot(grad_rows, weight_cols.T, preferred_element_type=jnp.float32)


def reference(out_grad, queries, enc_keys, enc_values, key_mask, weights):
    row_count = MB * BATCH * LEN
    feature_width = HEADS * HDIM
    ctx_grad = jnp.dot(out_grad.reshape(row_count, D), weights[1, 0], preferred_element_type=jnp.float32).astype(jnp.bfloat16)
    shaped = (MB * BATCH, LEN, HEADS, HDIM)
    query_grad, key_grad, value_grad = lax.map(attention_grads, (ctx_grad.reshape(shaped), queries.reshape(shaped), enc_keys.reshape(shaped), enc_values.reshape(shaped), key_mask.reshape(MB * BATCH, LEN)))
    query_grad = query_grad.reshape(row_count, feature_width)
    key_grad = key_grad.reshape(row_count, feature_width)
    value_grad = value_grad.reshape(row_count, feature_width)
    group_width = HEADS_DEV * HDIM
    dec_total = jnp.zeros((row_count, D), jnp.float32)
    enc_total = jnp.zeros((row_count, D), jnp.float32)
    for group_index in range(N_SEGMENT):
        low = group_index * group_width
        high = low + group_width
        dec_part = project(query_grad[:, low:high], weights[1, 1][:, low:high])
        enc_part = project(key_grad[:, low:high], weights[0, 0][:, low:high]) + project(value_grad[:, low:high], weights[0, 1][:, low:high])
        dec_total = dec_total + lax.optimization_barrier(dec_part.astype(jnp.bfloat16)).astype(jnp.float32)
        enc_total = enc_total + lax.optimization_barrier(enc_part.astype(jnp.bfloat16)).astype(jnp.float32)
    stacked = jnp.stack([enc_total, dec_total]).astype(jnp.bfloat16)
    return stacked.reshape(2, MB, BATCH, LEN, D)
```

```python
import functools

import jax
import jax.numpy as jnp
from jax import lax
from jax.experimental import pallas as pl
from jax.experimental.pallas import tpu as pltpu
from jax.sharding import PartitionSpec as P

HDIM = 128


def head_grads(mask_ref, grad_ref, query_ref, key_ref, value_ref, dq_ref, dk_ref, dv_ref):
    scale = HDIM ** (-0.5)
    f32 = jnp.float32

    def rows_rows(a, b):
        return lax.dot_general(a, b, (((1,), (1,)), ((), ())), preferred_element_type=f32)

    def cols_rows(a, b):
        return lax.dot_general(a, b, (((0,), (0,)), ((), ())), preferred_element_type=f32)

    grad, query, key, value = grad_ref[...], query_ref[...], key_ref[...], value_ref[...]
    scores = rows_rows(query, key) * scale
    scores = jnp.where(mask_ref[...] > 0, scores, -jnp.inf)
    exp_scores = jnp.exp(scores - jnp.max(scores, axis=-1, keepdims=True))
    probs = exp_scores / jnp.sum(exp_scores, axis=-1, keepdims=True)
    prob_grad = rows_rows(grad, value)
    center = jnp.sum(probs * prob_grad, axis=-1, keepdims=True)
    score_grad = (probs * (prob_grad - center)).astype(jnp.bfloat16)
    dq = jnp.dot(score_grad, key, preferred_element_type=f32) * scale
    dq_ref[...] = dq.astype(dq_ref.dtype)
    dk_ref[...] = (cols_rows(score_grad, query) * scale).astype(dk_ref.dtype)
    dv_ref[...] = cols_rows(probs.astype(jnp.bfloat16), grad).astype(dv_ref.dtype)


def attend(grad, queries, enc_keys, enc_values, key_mask):
    rows, width = grad.shape
    reactions, _, length = key_mask.shape
    heads = width // HDIM
    block = pl.BlockSpec((length, HDIM), lambda r, h: (r, h))
    return pl.pallas_call(
        head_grads,
        grid=(reactions, heads),
        in_specs=[pl.BlockSpec((None, 1, length), lambda r, h: (r, 0, 0))] + [block] * 4,
        out_specs=[block] * 3,
        out_shape=[jax.ShapeDtypeStruct((rows, width), jnp.bfloat16)] * 3,
        cost_estimate=pl.CostEstimate(
            flops=10 * rows * length * width,
            bytes_accessed=14 * rows * width,
            transcendentals=rows * length * heads,
        ),
    )(key_mask, grad, queries, enc_keys, enc_values)


def project(grad_rows, weight_cols):
    return lax.dot_general(
        grad_rows, weight_cols, (((1,), (1,)), ((), ())), preferred_element_type=jnp.float32
    )


def per_device(out_grad, queries, enc_keys, enc_values, key_mask, weights):
    section = lax.axis_index("section")
    decoder = section == 1
    segment = lax.axis_index("segment")
    segments, shards = lax.axis_size("segment"), lax.axis_size("fsdp")
    micro_count, reactions, length, features = out_grad.shape
    shard_rows, width = weights.shape[2:]
    half = width // 2
    piece = length // segments
    rows = shards * reactions * length

    first_half = lax.ppermute(weights[0, 0, :, :half], "section", [(1, 0)])
    own_weight = jnp.where(decoder, weights[0, 0, :, half:], first_half)

    def own_half(array):
        return lax.dynamic_slice_in_dim(array, section * half, half, axis=array.ndim - 1)

    results = []
    for micro in range(micro_count):
        piece_grad = lax.dynamic_slice_in_dim(out_grad[micro], segment * piece, piece, axis=1)
        moved = lax.all_to_all(piece_grad, "fsdp", split_axis=2, concat_axis=0, tiled=True)
        spread = lax.all_gather(moved, "segment", axis=0)
        spread = spread.reshape(segments * shards * reactions * piece, shard_rows)
        partial = jnp.dot(spread, own_weight, preferred_element_type=jnp.float32)
        partial = partial.astype(jnp.bfloat16)
        partial = partial.reshape(segments, shards * reactions, piece, half).transpose(1, 0, 2, 3)
        ctx_grad = lax.psum_scatter(
            partial.reshape(rows, half), "fsdp", scatter_dimension=0, tiled=True
        )
        flat = (reactions * length, half)
        query_grad, key_grad, value_grad = attend(
            ctx_grad,
            own_half(queries[micro]).reshape(flat),
            own_half(enc_keys[micro]).reshape(flat),
            own_half(enc_values[micro]).reshape(flat),
            key_mask[micro][:, None, :],
        )
        all_values = lax.all_gather(value_grad, "fsdp", axis=0, tiled=True)
        received = lax.ppermute(
            jnp.where(decoder, key_grad, query_grad), "section", [(0, 1), (1, 0)]
        )
        first = jnp.where(decoder, received, key_grad)
        second = jnp.where(decoder, query_grad, received)
        all_first = lax.all_gather(
            jnp.concatenate([first, second], axis=1), "fsdp", axis=0, tiled=True
        )
        other_values = lax.ppermute(all_values, "section", [(1, 0)])

        def decoder_part():
            return project(all_first, weights[0, 1]).astype(jnp.bfloat16)

        def encoder_part():
            values = jnp.concatenate([all_values, other_values], axis=1)
            total = project(all_first, weights[0, 0]) + project(values, weights[0, 1])
            return total.astype(jnp.bfloat16)

        part = lax.cond(decoder, decoder_part, encoder_part)
        part = part.reshape(shards * reactions, segments, piece, shard_rows).transpose(1, 0, 2, 3)
        part = part.reshape(segments * shards * reactions * piece, shard_rows)
        summed = lax.psum_scatter(part, "segment", scatter_dimension=0, tiled=True)
        summed = summed.reshape(shards * reactions, piece, shard_rows)
        summed = lax.all_to_all(summed, "fsdp", split_axis=0, concat_axis=2, tiled=True)
        summed = lax.all_to_all(summed, "segment", split_axis=2, concat_axis=1, tiled=True)
        results.append(summed)
    return jnp.stack(results)[None]


def solution(mesh):
    return jax.shard_map(
        per_device,
        mesh=mesh,
        in_specs=(
            P(None, "fsdp", None, None),
            P(None, "fsdp", None, "segment"),
            P(None, "fsdp", None, "segment"),
            P(None, "fsdp", None, "segment"),
            P(None, "fsdp", None),
            P("section", None, "fsdp", "segment"),
        ),
        out_specs=P("section", None, "fsdp", None, "segment"),
        check_vma=False,
    )
```

```python
import functools

import jax
import jax.numpy as jnp
from jax import lax
from jax.experimental import pallas as pl
from jax.experimental.pallas import tpu as pltpu
from jax.sharding import PartitionSpec as P

HDIM = 128


def head_grads(mask_ref, grad_ref, query_ref, key_ref, value_ref, dq_ref, dk_ref, dv_ref):
    scale = HDIM ** (-0.5)
    f32 = jnp.float32

    def rows_rows(a, b):
        return lax.dot_general(a, b, (((1,), (1,)), ((), ())), preferred_element_type=f32)

    def cols_rows(a, b):
        return lax.dot_general(a, b, (((0,), (0,)), ((), ())), preferred_element_type=f32)

    grad, query, key, value = grad_ref[...], query_ref[...], key_ref[...], value_ref[...]
    scores = rows_rows(query, key) * scale
    scores = jnp.where(mask_ref[...] > 0, scores, -jnp.inf)
    exp_scores = jnp.exp(scores - jnp.max(scores, axis=-1, keepdims=True))
    probs = exp_scores / jnp.sum(exp_scores, axis=-1, keepdims=True)
    prob_grad = rows_rows(grad, value)
    center = jnp.sum(probs * prob_grad, axis=-1, keepdims=True)
    score_grad = (probs * (prob_grad - center)).astype(jnp.bfloat16)
    dq = jnp.dot(score_grad, key, preferred_element_type=f32) * scale
    dq_ref[...] = dq.astype(dq_ref.dtype)
    dk_ref[...] = (cols_rows(score_grad, query) * scale).astype(dk_ref.dtype)
    dv_ref[...] = cols_rows(probs.astype(jnp.bfloat16), grad).astype(dv_ref.dtype)


def attend(grad, queries, enc_keys, enc_values, key_mask):
    rows, width = grad.shape
    reactions, _, length = key_mask.shape
    heads = width // HDIM
    block = pl.BlockSpec((length, HDIM), lambda r, h: (r, h))
    return pl.pallas_call(
        head_grads,
        grid=(reactions, heads),
        in_specs=[pl.BlockSpec((None, 1, length), lambda r, h: (r, 0, 0))] + [block] * 4,
        out_specs=[block] * 3,
        out_shape=[jax.ShapeDtypeStruct((rows, width), jnp.bfloat16)] * 3,
        cost_estimate=pl.CostEstimate(
            flops=10 * rows * length * width,
            bytes_accessed=14 * rows * width,
            transcendentals=rows * length * heads,
        ),
    )(key_mask, grad, queries, enc_keys, enc_values)


def project(grad_rows, weight_cols):
    return lax.dot_general(
        grad_rows, weight_cols, (((1,), (1,)), ((), ())), preferred_element_type=jnp.float32
    )


def per_device(out_grad, queries, enc_keys, enc_values, key_mask, weights):
    section = lax.axis_index("section")
    decoder = section == 1
    segment = lax.axis_index("segment")
    segments, shards = lax.axis_size("segment"), lax.axis_size("fsdp")
    micro_count, reactions, length, features = out_grad.shape
    shard_rows, width = weights.shape[2:]
    half = width // 2
    piece = length // segments
    rows = shards * reactions * length

    rows_cut = shard_rows // 2
    sent_rows = [
        lax.ppermute(weights[0, 0, :rows_cut, :half], "section", [(1, 0)]),
        lax.ppermute(weights[0, 0, rows_cut:, :half], "section", [(1, 0)]),
    ]

    def own_half(array):
        return lax.dynamic_slice_in_dim(array, section * half, half, axis=array.ndim - 1)

    def across(array, axis):
        return lax.all_to_all(array, axis, split_axis=0, concat_axis=0, tiled=True)

    moved_list = []
    for micro in range(micro_count):
        piece_grad = lax.dynamic_slice_in_dim(out_grad[micro], segment * piece, piece, axis=1)
        piece_grad = piece_grad.reshape(reactions * piece, shards, shard_rows).transpose(1, 0, 2)
        moved_list.append(across(piece_grad, "fsdp"))
    moved_list[0], sent_rows[0] = lax.optimization_barrier((moved_list[0], sent_rows[0]))
    spread_list = [lax.all_gather(moved, "segment", axis=0) for moved in moved_list]
    spread_list[0], sent_rows[1] = lax.optimization_barrier((spread_list[0], sent_rows[1]))
    own_weight = jnp.where(
        decoder, weights[0, 0, :, half:], jnp.concatenate(sent_rows, axis=0)
    )

    results = []
    for micro in range(micro_count):
        spread = spread_list[micro].reshape(rows, shard_rows)
        partial = jnp.dot(spread, own_weight, preferred_element_type=jnp.float32)
        partial = partial.astype(jnp.bfloat16)
        partial = partial.reshape(segments, shards * reactions, piece, half).transpose(1, 0, 2, 3)
        ctx_grad = lax.psum_scatter(
            partial.reshape(rows, half), "fsdp", scatter_dimension=0, tiled=True
        )
        flat = (reactions * length, half)
        query_grad, key_grad, value_grad = attend(
            ctx_grad,
            own_half(queries[micro]).reshape(flat),
            own_half(enc_keys[micro]).reshape(flat),
            own_half(enc_values[micro]).reshape(flat),
            key_mask[micro][:, None, :],
        )
        all_values = lax.all_gather(value_grad, "fsdp", axis=0, tiled=True)
        received = lax.ppermute(
            jnp.where(decoder, key_grad, query_grad), "section", [(0, 1), (1, 0)]
        )
        first = jnp.where(decoder, received, key_grad)
        second = jnp.where(decoder, query_grad, received)
        all_first = lax.all_gather(
            jnp.concatenate([first, second], axis=1), "fsdp", axis=0, tiled=True
        )
        other_values = lax.ppermute(all_values, "section", [(1, 0)])

        def decoder_part():
            return project(all_first, weights[0, 1]).astype(jnp.bfloat16)

        def encoder_part():
            values = jnp.concatenate([all_values, other_values], axis=1)
            total = project(all_first, weights[0, 0]) + project(values, weights[0, 1])
            return total.astype(jnp.bfloat16)

        part = lax.cond(decoder, decoder_part, encoder_part)
        part = part.reshape(shards * reactions, segments, piece, shard_rows).transpose(1, 0, 2, 3)
        part = part.reshape(segments * shards * reactions * piece, shard_rows)
        summed = lax.psum_scatter(part, "segment", scatter_dimension=0, tiled=True)
        summed = across(summed.reshape(shards, reactions * piece, shard_rows), "fsdp")
        summed = summed.transpose(1, 0, 2).reshape(reactions * piece, segments, features // segments)
        summed = across(summed.transpose(1, 0, 2), "segment")
        summed = summed.reshape(segments, reactions, piece, features // segments)
        summed = summed.transpose(1, 0, 2, 3)
        results.append(summed.reshape(reactions, length, features // segments))
    return jnp.stack(results)[None]


def solution(mesh):
    return jax.shard_map(
        per_device,
        mesh=mesh,
        in_specs=(
            P(None, "fsdp", None, None),
            P(None, "fsdp", None, "segment"),
            P(None, "fsdp", None, "segment"),
            P(None, "fsdp", None, "segment"),
            P(None, "fsdp", None),
            P("section", None, "fsdp", "segment"),
        ),
        out_specs=P("section", None, "fsdp", None, "segment"),
        check_vma=False,
    )
```

```python
import functools

import jax
import jax.numpy as jnp
from jax import lax
from jax.experimental import pallas as pl
from jax.experimental.pallas import tpu as pltpu
from jax.sharding import PartitionSpec as P

HDIM = 128


def head_grads(mask_ref, grad_ref, query_ref, key_ref, value_ref, dq_ref, dk_ref, dv_ref):
    scale = HDIM ** (-0.5)
    f32 = jnp.float32

    def rows_rows(a, b):
        return lax.dot_general(a, b, (((1,), (1,)), ((), ())), preferred_element_type=f32)

    def cols_rows(a, b):
        return lax.dot_general(a, b, (((0,), (0,)), ((), ())), preferred_element_type=f32)

    grad, query, key, value = grad_ref[...], query_ref[...], key_ref[...], value_ref[...]
    scores = rows_rows(query, key) * scale
    scores = jnp.where(mask_ref[...] > 0, scores, -jnp.inf)
    exp_scores = jnp.exp(scores - jnp.max(scores, axis=-1, keepdims=True))
    probs = exp_scores / jnp.sum(exp_scores, axis=-1, keepdims=True)
    prob_grad = rows_rows(grad, value)
    center = jnp.sum(probs * prob_grad, axis=-1, keepdims=True)
    score_grad = (probs * (prob_grad - center)).astype(jnp.bfloat16)
    dq = jnp.dot(score_grad, key, preferred_element_type=f32) * scale
    dq_ref[...] = dq.astype(dq_ref.dtype)
    dk_ref[...] = (cols_rows(score_grad, query) * scale).astype(dk_ref.dtype)
    dv_ref[...] = cols_rows(probs.astype(jnp.bfloat16), grad).astype(dv_ref.dtype)


def attend(grad, queries, enc_keys, enc_values, key_mask):
    rows, width = grad.shape
    reactions, _, length = key_mask.shape
    heads = width // HDIM
    block = pl.BlockSpec((length, HDIM), lambda r, h: (r, h))
    return pl.pallas_call(
        head_grads,
        grid=(reactions, heads),
        in_specs=[pl.BlockSpec((None, 1, length), lambda r, h: (r, 0, 0))] + [block] * 4,
        out_specs=[block] * 3,
        out_shape=[jax.ShapeDtypeStruct((rows, width), jnp.bfloat16)] * 3,
        cost_estimate=pl.CostEstimate(
            flops=10 * rows * length * width,
            bytes_accessed=14 * rows * width,
            transcendentals=rows * length * heads,
        ),
    )(key_mask, grad, queries, enc_keys, enc_values)


def project(grad_rows, weight_cols):
    return lax.dot_general(
        grad_rows, weight_cols, (((1,), (1,)), ((), ())), preferred_element_type=jnp.float32
    )


def per_device(out_grad, queries, enc_keys, enc_values, key_mask, weights):
    section = lax.axis_index("section")
    decoder = section == 1
    segment = lax.axis_index("segment")
    segments, shards = lax.axis_size("segment"), lax.axis_size("fsdp")
    micro_count, reactions, length, features = out_grad.shape
    shard_rows, width = weights.shape[2:]
    half = width // 2
    piece = length // segments
    rows = shards * reactions * length

    rows_cut = shard_rows // 2
    sent_rows = [
        lax.ppermute(weights[0, 0, :rows_cut, :half], "section", [(1, 0)]),
        lax.ppermute(weights[0, 0, rows_cut:, :half], "section", [(1, 0)]),
    ]

    def own_half(array):
        return lax.dynamic_slice_in_dim(array, section * half, half, axis=array.ndim - 1)

    def across(array, axis):
        return lax.all_to_all(array, axis, split_axis=0, concat_axis=0, tiled=True)

    pieces = []
    for micro in range(micro_count):
        piece_grad = lax.dynamic_slice_in_dim(out_grad[micro], segment * piece, piece, axis=1)
        pieces.append(
            piece_grad.reshape(reactions * piece, shards, shard_rows).transpose(1, 0, 2)
        )
    moved_list = []
    for micro in range(micro_count):
        moved_list.append(across(pieces[micro], "fsdp"))
        if micro < 2:
            moved_list[micro], sent_rows[micro] = lax.optimization_barrier(
                (moved_list[micro], sent_rows[micro])
            )
    own_weight = jnp.where(
        decoder, weights[0, 0, :, half:], jnp.concatenate(sent_rows, axis=0)
    )

    grads_list = []
    for micro in range(micro_count):
        moved = moved_list[micro]
        if micro == 0:
            spread = lax.all_gather(moved, "segment", axis=0)
        else:
            moved, _ = lax.optimization_barrier((moved, partial))
            spread = across(jnp.broadcast_to(moved[None], (segments,) + moved.shape), "segment")
        partial = jnp.dot(
            spread.reshape(rows, shard_rows), own_weight, preferred_element_type=jnp.float32
        ).astype(jnp.bfloat16)
        partial = partial.reshape(segments, shards * reactions, piece, half).transpose(1, 0, 2, 3)
        partial = partial.reshape(rows, half)
        ctx_grad = lax.psum_scatter(partial, "fsdp", scatter_dimension=0, tiled=True)
        flat = (reactions * length, half)
        query_grad, key_grad, value_grad = attend(
            ctx_grad,
            own_half(queries[micro]).reshape(flat),
            own_half(enc_keys[micro]).reshape(flat),
            own_half(enc_values[micro]).reshape(flat),
            key_mask[micro][:, None, :],
        )
        received = lax.ppermute(
            jnp.where(decoder, key_grad, query_grad), "section", [(0, 1), (1, 0)]
        )
        first = jnp.where(decoder, received, key_grad)
        second = jnp.where(decoder, query_grad, received)
        grads_list.append((first, second, value_grad))

    gathered_list = []
    for micro in range(micro_count):
        first, second, value_grad = grads_list[micro]
        all_values = lax.all_gather(value_grad, "fsdp", axis=0, tiled=True)
        all_first = lax.all_gather(
            jnp.concatenate([first, second], axis=1), "fsdp", axis=0, tiled=True
        )
        other_values = lax.ppermute(all_values, "section", [(1, 0)])
        gathered_list.append((all_first, all_values, other_values))

    results = []
    for micro in range(micro_count):
        all_first, all_values, other_values = gathered_list[micro]

        def no_values():
            return jnp.zeros((rows, shard_rows), jnp.float32)

        def values_part():
            values = jnp.concatenate([all_values, other_values], axis=1)
            return project(values, weights[0, 1])

        from_values = lax.cond(decoder, no_values, values_part)
        if micro > 0:
            all_first, results[-1], from_values = lax.optimization_barrier(
                (all_first, results[-1], from_values)
            )

        def decoder_part():
            return project(all_first, weights[0, 1]).astype(jnp.bfloat16)

        def encoder_part():
            return (project(all_first, weights[0, 0]) + from_values).astype(jnp.bfloat16)

        part = lax.cond(decoder, decoder_part, encoder_part)
        part = part.reshape(shards * reactions, segments, piece, shard_rows).transpose(1, 0, 2, 3)
        part = across(part.reshape(segments, shards * reactions * piece, shard_rows), "segment")
        summed = jnp.sum(part.astype(jnp.float32), axis=0).astype(jnp.bfloat16)
        summed = across(summed.reshape(shards, reactions * piece, shard_rows), "fsdp")
        summed = summed.transpose(1, 0, 2).reshape(reactions * piece, segments, features // segments)
        summed = across(summed.transpose(1, 0, 2), "segment")
        summed = summed.reshape(segments, reactions, piece, features // segments)
        summed = summed.transpose(1, 0, 2, 3)
        results.append(summed.reshape(reactions, length, features // segments))
    return jnp.stack(results)[None]


def solution(mesh):
    return jax.shard_map(
        per_device,
        mesh=mesh,
        in_specs=(
            P(None, "fsdp", None, None),
            P(None, "fsdp", None, "segment"),
            P(None, "fsdp", None, "segment"),
            P(None, "fsdp", None, "segment"),
            P(None, "fsdp", None),
            P("section", None, "fsdp", "segment"),
        ),
        out_specs=P("section", None, "fsdp", None, "segment"),
        check_vma=False,
    )
```
